256 devices in a mesh: dp: 2 (over core), space: 32 (over z, x), feat: 4 (over y).
Axes of the slice: x: 4, y: 4, z: 8, core: 2. Of those that a mesh axis runs over, the one named last changes fastest.
Arguments:
- patches: bfloat16 [4, 192, 360, 1280], P('dp', 'space', 'feat'), parts along dimension 0, may hold values from -6 to 6
- embed_weight: bfloat16 [1280, 1024], replicated
- embed_bias: float32 [1024], replicated
- norm_gain: float32 [1024], replicated, may hold values from 0.1 to 1.9
- norm_bias: float32 [1024], replicated, may hold values from -2 to 2
- w_one: float32 [2, 8, 128, 128], P(None, 'feat'), may hold values from -0.375 to 0.375
- b_one: float32 [2, 8, 128], P(None, 'feat'), may hold values from -3 to 3
- w_two: float32 [2, 8, 128, 128], P(None, 'feat'), may hold values from -0.375 to 0.375
- b_two: float32 [2, 8, 128], P(None, 'feat'), may hold values from -0.6 to 0.6
- lat_cut: int32 [8], P('feat'), may hold values from 32 to 64, as said below
- lon_cut: int32 [8], P('feat'), may hold values from 64 to 128, as said below
Outputs:
- mixed: bfloat16 [4, 192, 360, 1024], P('dp', 'space', None, 'feat'), parts along dimension 0
The draws below stay inside these ranges and needn't reach their ends.
There are 2 independent parts, one for each index of `dp`. The reference program is written for one: setup_inputs(seed, part) draws one part's arguments, and reference() takes and returns one part's arrays. A program takes and returns all parts, laid end to end along the dimension named above; an argument that names none is the same for every part. Nothing has to cross between parts.
Inputs may be any that keep to these rules, and one draw needn't show every extreme that they name: `lat_cut`: some block has bound exactly 64. `lon_cut`: some block has bound exactly 128.
All inputs are finite; a program needn't handle non-finite values.
Results may differ from the reference program's by a relative error of at most 0.0065.
Values may be sent and summed in bfloat16 or wider, within the bound.
A program may use at most 128 MiB of HBM per device.

```python
import jax
import jax.numpy as jnp
from jax import lax

SAMPLES = 2
H = 192
W = 360
PATCH = 1280
D = 1024
BLOCKS = 8
KEEP_LAT = 64
KEEP_LON = 128
BS = 128


def cutoff_draw(key, largest):
    values = jax.random.randint(key, (BLOCKS,), largest // 2, largest + 1).astype(jnp.int32)
    chosen = jax.random.randint(jax.random.fold_in(key, 11), (), 0, BLOCKS)
    return jnp.where(jnp.arange(BLOCKS) == chosen, largest, values).astype(jnp.int32)


def draw_lat_cut(key, part):
    key = jax.random.fold_in(key, 3)
    return cutoff_draw(key, KEEP_LAT)


def draw_lon_cut(key, part):
    key = jax.random.fold_in(key, 5)
    return cutoff_draw(key, KEEP_LON)


def draw_embed_weight(key, part):
    key = jax.random.fold_in(key, 7)
    position = jnp.arange(D, dtype=jnp.float32) / (D - 1)
    entries = jnp.clip(jax.random.normal(key, (PATCH, D), jnp.float32), -6.0, 6.0)
    column_scale = 0.5 * jnp.exp(position * 1.0986123)
    return (entries * column_scale[None, :] * PATCH ** (-0.5)).astype(jnp.bfloat16)


def draw_embed_bias(key, part):
    key = jax.random.fold_in(key, 9)
    position = jnp.arange(D, dtype=jnp.float32) / (D - 1)
    rough = 0.3 * jnp.clip(jax.random.normal(key, (D,), jnp.float32), -3.0, 3.0)
    ramp = -1.5 + 3.0 * position
    return (ramp + rough).astype(jnp.float32)


def levels(own_key, extent, cuts, low, high):
    def one(axis_at, shards_of):
        draws = jax.random.uniform(jax.random.fold_in(jax.random.fold_in(own_key, 6), axis_at), (shards_of,), jnp.float32, low / len(cuts), high / len(cuts))
        return jnp.repeat(jnp.exp(draws), extent[axis_at] // shards_of).reshape((-1,) + (1,) * (len(extent) - axis_at - 1))

    factor_of = one(*cuts[0])
    for cut in cuts[1:]:
        factor_of = factor_of * one(*cut)
    return factor_of


def gaussian(key, extent, width, limit, pieces=(), held_as=jnp.bfloat16):
    values = jax.random.normal(key, extent, jnp.float32) * width
    if len(pieces) > 0:
        values = levels(key, extent, pieces, -0.22, 0.18) * values
    return jnp.clip(values, min=-limit, max=limit).astype(held_as)


def setup_inputs(seed: int = 0, part: int = 0) -> dict:
    splits = jax.random.split(jax.random.key(seed), 12)
    part_splits = jax.random.split(jax.random.fold_in(splits[11], part), 12)
    return {
        "patches": gaussian(part_splits[0], (SAMPLES, H, W, PATCH), 1.0, 6.0, ((1, 32), (2, 4))),
        "embed_weight": draw_embed_weight(jax.random.fold_in(splits[11], 71), part),
        "embed_bias": draw_embed_bias(jax.random.fold_in(splits[11], 71), part),
        "norm_gain": jnp.clip(1.0 + 0.18 * jax.random.normal(splits[3], (D,), jnp.float32), 0.1, 1.9),
        "norm_bias": gaussian(splits[4], (D,), 0.3, 2.0, (), jnp.float32),
        "w_one": gaussian(splits[5], (2, BLOCKS, BS, BS), (2 * BS) ** -0.5, 0.375, ((1, 4),), jnp.float32),
        "b_one": gaussian(splits[6], (2, BLOCKS, BS), 0.5, 3.0, ((1, 4),), jnp.float32),
        "w_two": gaussian(splits[7], (2, BLOCKS, BS, BS), (2 * BS) ** -0.5, 0.375, ((1, 4),), jnp.float32),
        "b_two": gaussian(splits[8], (2, BLOCKS, BS), 0.1, 0.6, ((1, 4),), jnp.float32),
        "lat_cut": draw_lat_cut(jax.random.fold_in(splits[11], 71), part),
        "lon_cut": draw_lon_cut(jax.random.fold_in(splits[11], 71), part),
    }


SHRINK = 0.01
EPSILON = 1e-05

def block_apply(real_in, imag_in, weight, bias_re, bias_im):

    def mult(values, matrix):
        return jnp.einsum('...kc,kcd->...kd', values, matrix, precision=lax.Precision.HIGHEST)
    out_re = mult(real_in, weight[0]) - mult(imag_in, weight[1]) + bias_re
    out_im = mult(imag_in, weight[0]) + mult(real_in, weight[1]) + bias_im
    return (out_re, out_im)

def block_mlp(real_in, imag_in, w_one, b_one, w_two, b_two):
    first_re, first_im = block_apply(real_in, imag_in, w_one, b_one[0], b_one[1])
    first_re = jax.nn.relu(first_re)
    first_im = jax.nn.relu(first_im)
    second_re, second_im = block_apply(first_re, first_im, w_two, b_two[0], b_two[1])
    second_re = second_re - jnp.clip(second_re, -SHRINK, SHRINK)
    second_im = second_im - jnp.clip(second_im, -SHRINK, SHRINK)
    return (second_re, second_im)

def reference(patches, embed_weight, embed_bias, norm_gain, norm_bias, w_one, b_one, w_two, b_two, lat_cut, lon_cut):
    lat_freq = jnp.concatenate([jnp.arange(KEEP_LAT, dtype=jnp.int32), jnp.arange(-KEEP_LAT, 0, dtype=jnp.int32)])
    lon_freq = jnp.arange(KEEP_LON, dtype=jnp.int32)
    keep_mask = (jnp.abs(lat_freq)[:, None, None] < lat_cut[None, None, :]) & (lon_freq[None, :, None] < lon_cut[None, None, :])
    keep_mask = keep_mask.astype(jnp.float32)[..., None]
    dc_mask = (jnp.arange(KEEP_LON) > 0).astype(jnp.float32)[None, :, None]

    def one_sample(sample):
        embedded = jnp.dot(sample.reshape(-1, PATCH), embed_weight, preferred_element_type=jnp.float32).reshape(H, W, D) + embed_bias
        mean_value = lax.optimization_barrier(jnp.mean(embedded, axis=-1, keepdims=True))
        centred = embedded - mean_value
        variance = lax.optimization_barrier(jnp.mean(centred * centred, axis=-1, keepdims=True))
        normed = (centred * lax.rsqrt(variance + EPSILON) * norm_gain + norm_bias).astype(jnp.bfloat16)
        spectrum = jnp.fft.rfft2(normed.astype(jnp.float32), axes=(0, 1), norm='ortho')
        kept = jnp.concatenate([spectrum[:KEEP_LAT, :KEEP_LON], spectrum[H - KEEP_LAT:, :KEEP_LON]], axis=0)
        shape_blocks = (2 * KEEP_LAT, KEEP_LON, BLOCKS, BS)
        real_in = jnp.real(kept).reshape(shape_blocks)
        imag_in = jnp.imag(kept).reshape(shape_blocks)
        out_re, out_im = block_mlp(real_in, imag_in, w_one, b_one, w_two, b_two)
        out_re = (out_re * keep_mask).reshape(2 * KEEP_LAT, KEEP_LON, D)
        out_im = (out_im * keep_mask).reshape(2 * KEEP_LAT, KEEP_LON, D)
        middle = jnp.zeros((H - 2 * KEEP_LAT, KEEP_LON, D), out_re.dtype)
        full_re = jnp.concatenate([out_re[:KEEP_LAT], middle, out_re[KEEP_LAT:]], axis=0)
        full_im = jnp.concatenate([out_im[:KEEP_LAT], middle, out_im[KEEP_LAT:]], axis=0)
        rows = jnp.fft.ifft(lax.complex(full_re, full_im), axis=0, norm='ortho')
        rows_re = jnp.real(rows)
        rows_im = jnp.imag(rows) * dc_mask
        tail = jnp.zeros((H, W // 2 + 1 - KEEP_LON, D), rows_re.dtype)
        padded = lax.complex(jnp.concatenate([rows_re, tail], axis=1), jnp.concatenate([rows_im, tail], axis=1))
        filtered = jnp.fft.irfft(padded, n=W, axis=1, norm='ortho')
        return (embedded + filtered).astype(jnp.bfloat16)
    return lax.map(one_sample, patches)
```

```python
import math

import jax
import jax.numpy as jnp
import ml_dtypes
import numpy as np
from jax import lax
from jax.experimental import pallas as pl
from jax.experimental.pallas import tpu as pltpu
from jax.sharding import PartitionSpec as P

MESH = pl.DeviceIdType.MESH
BF = jnp.bfloat16
F32 = jnp.float32

SAMPLES, H, W = 2, 192, 360
PATCH, D = 1280, 1024
KEEP_LAT, KEEP_LON = 64, 128
SHRINK = 0.01
EPSILON = 1e-05

NZ, NX, NY = 8, 4, 4
RS = H // (NZ * NX)
ROWS = SAMPLES * RS
COLS = W // NY
PAD = 96
CH = D // NY
MODES = KEEP_LON // (NZ * NX)
LAG = 5
FWD = 5
STEP = 2


def split(table):
    high = table.astype(ml_dtypes.bfloat16)
    low = (table - high.astype(np.float64)).astype(ml_dtypes.bfloat16)
    return high, low


def phase_tables():
    lon = np.full((NY, PAD), 0)
    for q in range(NY):
        lon[q, :COLS] = q * COLS + np.arange(COLS)
    real_col = np.broadcast_to(np.arange(PAD) < COLS, (NY, PAD)).reshape(-1)
    lon = lon.reshape(-1)
    g = np.arange(KEEP_LON)
    ang = 2.0 * math.pi * ((g[:, None] * lon[None, :]) % W) / W
    fwd = np.stack([np.cos(ang), -np.sin(ang)], axis=1) * real_col / math.sqrt(W)
    fwd = fwd.reshape(2 * KEEP_LON, NY * PAD)
    gx = np.arange(KEEP_LON).reshape(NZ, NX, MODES).transpose(1, 0, 2).reshape(-1)
    ang = 2.0 * math.pi * ((lon[:, None] * gx[None, :]) % W) / W
    weight = np.where(gx == 0, 1.0, 2.0) / math.sqrt(W)
    inv = np.stack([np.cos(ang) * weight, -np.sin(ang) * weight], axis=2) * real_col[:, None, None]
    inv = inv.reshape(NY * PAD, 2 * KEEP_LON)
    lat = np.arange(H).reshape(NZ, NX, RS).transpose(1, 2, 0).reshape(-1)
    f = np.concatenate([np.arange(KEEP_LAT), np.arange(-KEEP_LAT, 0)])
    ang = 2.0 * math.pi * ((f[:, None] * lat[None, :]) % H) / H
    c, s = np.cos(ang) / math.sqrt(H), np.sin(ang) / math.sqrt(H)
    lat_fwd = np.concatenate([np.concatenate([c, s], 1), np.concatenate([-s, c], 1)], 0)
    c, s = c.T, s.T
    lat_inv = np.concatenate([np.concatenate([c, -s], 1), np.concatenate([s, c], 1)], 0)
    wide = np.stack([*split(fwd), *split(lat_fwd)])
    tall = np.stack([*split(lat_inv), *split(inv)])
    return wide, tall


def dot(a, b):
    return jnp.dot(a, b, preferred_element_type=F32)


def halves(value):
    high = value.astype(BF)
    return high, (value - high.astype(F32)).astype(BF)


def complex_weight(w_ref, k):
    re, im = w_ref[0, k], w_ref[1, k]
    return jnp.concatenate(
        [jnp.concatenate([re, im], axis=1), jnp.concatenate([-im, re], axis=1)], axis=0
    )


def kernel(
    p_hbm, w_hbm, eb_ref, gain_ref, shift_ref, w1_ref, b1_ref, w2_ref, b2_ref, latc, lonc, wide_hbm, tall_hbm,
    out_hbm,
    pbuf, wbuf, wide, tall, zs, zr, st, sb, zr1, xr1, rel, xs2, xr2, fr, ob, flat, w1h, w1l, w2h, w2l,
    pat_sem, wgt_sem, tab_sem, send_sem, y_sem, st_sem, z1_sem, x1_sem, x2_sem, z2_sem, out_sem,
):
    space = lax.axis_index("space")
    yi = lax.axis_index("feat")
    zi, xi = space // NX, lax.rem(space, NX)
    y_peer = lambda d: lax.rem(yi + d, NY)
    z_peer = lambda d: lax.rem(zi + d, NZ)
    x_peer = lambda d: lax.rem(xi + d, NX)
    y_id = lambda y: {"feat": y}
    z_id = lambda z: {"space": z * NX + xi}
    x_id = lambda x: {"space": zi * NX + x}
    Y_ORDER, X_ORDER, Z_ORDER = (2, 1, 3), (2, 1, 3), (4, 3, 5, 2, 6, 1, 7)

    def remote(src, dst, sends, recv, where):
        pltpu.make_async_remote_copy(
            src_ref=src, dst_ref=dst, send_sem=send_sem.at[sends], recv_sem=recv, device_id=where, device_id_type=MESH
        ).start()

    def patch_copy(r):
        return pltpu.make_async_copy(p_hbm.at[r], pbuf.at[r], pat_sem.at[r])

    patch_copy(0).start()
    weight_copy = pltpu.make_async_copy(w_hbm, wbuf, wgt_sem)
    weight_copy.start()

    barrier = pltpu.get_barrier_semaphore()
    for d in Y_ORDER:
        pl.semaphore_signal(barrier, inc=1, device_id=y_id(y_peer(d)), device_id_type=MESH)
    for d in Z_ORDER:
        pl.semaphore_signal(barrier, inc=1, device_id=z_id(z_peer(d)), device_id_type=MESH)
    for d in X_ORDER:
        pl.semaphore_signal(barrier, inc=1, device_id=x_id(x_peer(d)), device_id_type=MESH)

    @pl.loop(1, ROWS)
    def _(r):
        patch_copy(r).start()

    wide_copy = pltpu.make_async_copy(wide_hbm, wide, tab_sem.at[0])
    tall_copy = pltpu.make_async_copy(tall_hbm, tall, tab_sem.at[1])
    wide_copy.start()
    tall_copy.start()

    @pl.loop(0, ROWS)
    def _(r):
        for q in range(NY):
            zs[r, q, 80:, :] = jnp.zeros((PAD - 80, CH), BF)
        zr[r, yi, 80:, :] = jnp.zeros((PAD - 80, CH), BF)

    for k in range(2):
        w1h[k], w1l[k] = halves(complex_weight(w1_ref, k))
        w2h[k], w2l[k] = halves(complex_weight(w2_ref, k))
    st[yi] = jnp.zeros((PAD, 128), F32)
    lane = lax.broadcasted_iota(jnp.int32, (PAD, 128), 1)
    channels = pl.ds(pl.multiple_of(yi * CH, CH), CH)

    pl.semaphore_wait(barrier, len(Y_ORDER) + len(Z_ORDER) + len(X_ORDER))
    weight_copy.wait()

    def embed(r):
        patch_copy(r).wait()
        e = dot(pbuf[r], wbuf[...]) + eb_ref[...]
        mean = jnp.mean(e, axis=1, keepdims=True)
        e = e - mean
        var = jnp.mean(e * e, axis=1, keepdims=True) + EPSILON
        inv = lax.rsqrt(var)
        z = (e * inv).astype(BF)
        for q in range(NY):
            zs[r, q, 0:COLS, :] = z[:, q * CH : (q + 1) * CH]
        for d in Y_ORDER:
            remote(zs.at[r, y_peer(d)], zr.at[r, yi], 0, y_sem.at[r], y_id(y_peer(d)))
        zr[r, yi] = zs[r, yi]
        part = lane[0:COLS]
        old = st[yi, 0:COLS]
        st[yi, 0:COLS] = jnp.where(part == 2 * r, var * inv, jnp.where(part == 2 * r + 1, mean, old))

    def to_modes(r):
        pltpu.make_async_copy(zr.at[r, 0 : NY - 1], zr.at[r, 0 : NY - 1], y_sem.at[r]).wait()
        z = zr[r].reshape(NY * PAD, CH).astype(F32)
        n = (z * gain_ref[:, channels] + shift_ref[:, channels]).astype(BF)
        s = (dot(wide[0], n) + dot(wide[1], n)).reshape(NZ * NX, 2 * MODES, CH)
        s = jnp.concatenate([s[:, :, 0:128], s[:, :, 128:256]], axis=1).astype(BF)
        sb[r] = s.reshape(NZ, NX, 16, 128)
        for d in Z_ORDER:
            remote(sb.at[r, z_peer(d)], zr1.at[:, r, zi], 1, z1_sem.at[r], z_id(z_peer(d)))
        pltpu.make_async_copy(sb.at[r, zi], zr1.at[:, r, zi], z1_sem.at[r]).start()

    def pass_on(r):
        pltpu.make_async_copy(zr1.at[:, r], zr1.at[:, r], z1_sem.at[r]).wait()
        for d in X_ORDER:
            remote(zr1.at[x_peer(d), r], xr1.at[xi, r], 2, x1_sem.at[r], x_id(x_peer(d)))
        pltpu.make_async_copy(zr1.at[xi, r], xr1.at[xi, r], x1_sem.at[r]).start()

    def mix(s):
        rows = pl.ds(s * RS, RS)
        for i in range(RS):
            r = s * RS + i
            pltpu.make_async_copy(xr1.at[:, r], xr1.at[:, r], x1_sem.at[r]).wait()
        n = RS * NZ * 16
        for x in range(NX):
            rel[x * n : (x + 1) * n, :] = xr1[x, rows].astype(F32).reshape(n, 128)
        outs = []
        for k in range(2):
            cols = []
            for m in range(MODES):
                both = [rel[pl.ds(k * 8 + m * 2 + i, H, stride=16), :].astype(BF) for i in range(2)]
                cols.append(jnp.concatenate(both, axis=0))
            data = jnp.concatenate(cols, axis=1)
            g = dot(wide[2], data) + dot(wide[3], data)
            v = jnp.concatenate(
                [
                    jnp.concatenate([g[0:128, m * 128 : (m + 1) * 128], g[128:256, m * 128 : (m + 1) * 128]], axis=1)
                    for m in range(MODES)
                ],
                axis=0,
            )
            for first, (wh, wl, b_ref) in enumerate(((w1h, w1l, b1_ref), (w2h, w2l, b2_ref))):
                vh, vl = halves(v)
                bias = jnp.concatenate([b_ref[0, k : k + 1], b_ref[1, k : k + 1]], axis=1)
                v = dot(vh, wh[k]) + dot(vl, wh[k]) + dot(vh, wl[k]) + bias
                if first == 0:
                    v = jnp.maximum(v, 0.0)
            v = v - jnp.clip(v, -SHRINK, SHRINK)
            f = lax.broadcasted_iota(jnp.int32, (128, 1), 0)
            f = jnp.where(f < KEEP_LAT, f, 2 * KEEP_LAT - f)
            keep_lat = f < latc[k]
            cols = []
            for m in range(MODES):
                part = v[m * 128 : (m + 1) * 128]
                keep = jnp.logical_and(keep_lat, space * MODES + m < lonc[k])
                part = jnp.where(keep, part, 0.0)
                cols.append(jnp.concatenate([part[:, 0:128], part[:, 128:256]], axis=0))
            oh, ol = halves(jnp.concatenate(cols, axis=1))
            outs.append(dot(tall[0], oh) + dot(tall[1], oh) + dot(tall[0], ol))
        for k in range(2):
            for m in range(MODES):
                for i in range(2):
                    rel[pl.ds(k * 8 + m * 2 + i, H, stride=16), :] = outs[k][
                        i * H : (i + 1) * H, m * 128 : (m + 1) * 128
                    ]
        for x in range(NX):
            xs2[x, rows] = rel[x * n : (x + 1) * n, :].reshape(RS, NZ, 16, 128).astype(BF)
        for j in range(RS // STEP):
            some = pl.ds(s * RS + j * STEP, STEP)
            sem = x2_sem.at[s * (RS // STEP) + j]
            for d in X_ORDER:
                remote(xs2.at[x_peer(d), some], xr2.at[xi, some], 3, sem, x_id(x_peer(d)))
            pltpu.make_async_copy(xs2.at[xi, some], xr2.at[xi, some], sem).start()

    def send_back(j):
        some = pl.ds(j * STEP, STEP)
        pltpu.make_async_copy(xr2.at[:, some], xr2.at[:, some], x2_sem.at[j]).wait()
        for d in Z_ORDER:
            remote(xr2.at[:, some, z_peer(d)], fr.at[:, some, zi], 4, z2_sem.at[j], z_id(z_peer(d)))
        pltpu.make_async_copy(xr2.at[:, some, zi], fr.at[:, some, zi], z2_sem.at[j]).start()

    def out_copy(r):
        return pltpu.make_async_copy(ob.at[r], out_hbm.at[r], out_sem)

    def to_tokens(r):
        a = fr[:, r].astype(F32).reshape(NX * NZ, 16, 128)
        a = jnp.concatenate([a[:, 0:8], a[:, 8:16]], axis=2).reshape(2 * KEEP_LON, CH).astype(BF)
        filtered = dot(tall[2], a) + dot(tall[3], a)
        for q in range(NY):
            stat = st[q]
            std = jnp.sum(jnp.where(lane == 2 * r, stat, 0.0), axis=1, keepdims=True)
            mean = jnp.sum(jnp.where(lane == 2 * r + 1, stat, 0.0), axis=1, keepdims=True)
            mixed = filtered[q * PAD : (q + 1) * PAD] + (zr[r, q].astype(F32) * std + mean)
            flat[q * COLS : (q + 1) * COLS, :] = mixed[0:COLS]
        ob[r] = flat[...].astype(BF)
        out_copy(r).start()

    def finish(j):
        some = pl.ds(j * STEP, STEP)
        pltpu.make_async_copy(fr.at[:, some], fr.at[:, some], z2_sem.at[j]).wait()

        @pl.loop(0, STEP)
        def _(i):
            to_tokens(j * STEP + i)

    @pl.loop(0, ROWS + LAG)
    def _(i):
        @pl.when(i < ROWS)
        def _():
            embed(i)

        @pl.when(i == ROWS - 1)
        def _():
            for d in Y_ORDER:
                remote(st.at[yi], st.at[yi], 5, st_sem, y_id(y_peer(d)))

        @pl.when(i == LAG)
        def _():
            wide_copy.wait()

        @pl.when(i >= LAG)
        def _():
            to_modes(i - LAG)

        @pl.when(i >= LAG + FWD)
        def _():
            pass_on(i - LAG - FWD)

    tall_copy.wait()
    half = RS // STEP
    mix(0)

    @pl.loop(ROWS - FWD, ROWS)
    def _(r):
        pass_on(r)

    @pl.loop(0, half)
    def _(j):
        send_back(j)

    mix(1)
    pltpu.make_async_copy(st.at[0 : NY - 1], st.at[0 : NY - 1], st_sem).wait()
    finish(0)

    @pl.loop(half, 2 * half)
    def _(j):
        send_back(j)

    @pl.loop(1, 2 * half)
    def _(j):
        finish(j)

    for sends, ref in enumerate(
        (
            zs.at[:, 0 : NY - 1],
            sb.at[:, 0 : NZ - 1],
            zr1.at[0 : NX - 1],
            xs2.at[0 : NX - 1],
            xr2.at[:, :, 0 : NZ - 1],
            st.at[0 : NY - 1],
        )
    ):
        pltpu.make_async_copy(ref, ref, send_sem.at[sends]).wait()
    pltpu.make_async_copy(ob, out_hbm, out_sem).wait()


def solution(mesh):
    wide, tall = phase_tables()

    def local(
        patches, embed_weight, embed_bias, norm_gain, norm_bias, w_one, b_one, w_two, b_two, lat_cut, lon_cut
    ):
        anywhere = pl.BlockSpec(memory_space=pl.ANY)
        vmem = pl.BlockSpec(memory_space=pltpu.VMEM)
        smem = pl.BlockSpec(memory_space=pltpu.SMEM)
        back = (NX, ROWS, NZ, 16, 128)
        out = pl.pallas_call(
            kernel,
            out_shape=jax.ShapeDtypeStruct((ROWS, W, CH), BF),
            in_specs=[anywhere, anywhere] + [vmem] * 7 + [smem, smem, anywhere, anywhere],
            out_specs=anywhere,
            scratch_shapes=[
                pltpu.VMEM((ROWS, COLS, PATCH), BF),
                pltpu.VMEM((PATCH, D), BF),
                pltpu.VMEM((4, 256, 384), BF),
                pltpu.VMEM((4, 384, 256), BF),
                pltpu.VMEM((ROWS, NY, PAD, CH), BF),
                pltpu.VMEM((ROWS, NY, PAD, CH), BF),
                pltpu.VMEM((NY, PAD, 128), F32),
                pltpu.VMEM((ROWS, NZ, NX, 16, 128), BF),
                pltpu.VMEM(back, BF),
                pltpu.VMEM(back, BF),
                pltpu.VMEM((H * 16, 128), F32),
                pltpu.VMEM(back, BF),
                pltpu.VMEM(back, BF),
                pltpu.VMEM(back, BF),
                pltpu.VMEM((ROWS, W, CH), BF),
                pltpu.VMEM((W, CH), F32),
            ]
            + [pltpu.VMEM((2, 256, 256), BF)] * 4
            + [
                pltpu.SemaphoreType.DMA((ROWS,)),
                pltpu.SemaphoreType.DMA,
                pltpu.SemaphoreType.DMA((2,)),
                pltpu.SemaphoreType.DMA((6,)),
                pltpu.SemaphoreType.DMA((ROWS,)),
                pltpu.SemaphoreType.DMA,
                pltpu.SemaphoreType.DMA((ROWS,)),
                pltpu.SemaphoreType.DMA((ROWS,)),
                pltpu.SemaphoreType.DMA((ROWS // STEP,)),
                pltpu.SemaphoreType.DMA((ROWS // STEP,)),
                pltpu.SemaphoreType.DMA,
            ],
            compiler_params=pltpu.CompilerParams(
                collective_id=0, has_side_effects=True, vmem_limit_bytes=56 * 1024 * 1024
            ),
            name="afno",
        )(
            patches.reshape(ROWS, COLS, PATCH),
            embed_weight,
            embed_bias.reshape(1, D),
            norm_gain.reshape(1, D),
            norm_bias.reshape(1, D),
            w_one,
            b_one,
            w_two,
            b_two,
            lat_cut,
            lon_cut,
            jnp.asarray(wide),
            jnp.asarray(tall),
        )
        return out.reshape(SAMPLES, RS, W, CH)

    in_specs = (
        P("dp", "space", "feat", None),
        P(),
        P(),
        P(),
        P(),
        P(None, "feat", None, None),
        P(None, "feat", None),
        P(None, "feat", None, None),
        P(None, "feat", None),
        P("feat"),
        P("feat"),
    )
    return jax.shard_map(
        local, mesh=mesh, in_specs=in_specs, out_specs=P("dp", "space", None, "feat"), check_vma=False
    )
```

```python
import math

import jax
import jax.numpy as jnp
import ml_dtypes
import numpy as np
from jax import lax
from jax.experimental import pallas as pl
from jax.experimental.pallas import tpu as pltpu
from jax.sharding import PartitionSpec as P

MESH = pl.DeviceIdType.MESH
BF = jnp.bfloat16
F32 = jnp.float32

SAMPLES, H, W = 2, 192, 360
PATCH, D = 1280, 1024
KEEP_LAT, KEEP_LON = 64, 128
SHRINK = 0.01
EPSILON = 1e-05

NZ, NX, NY = 8, 4, 4
RS = H // (NZ * NX)
ROWS = SAMPLES * RS
COLS = W // NY
PAD = 96
CH = D // NY
MODES = KEEP_LON // (NZ * NX)
LANES = 128
PARTS = PATCH // LANES
LAG = 3
FWD = 5
STEP = 2


def split(table):
    high = table.astype(ml_dtypes.bfloat16)
    low = (table - high.astype(np.float64)).astype(ml_dtypes.bfloat16)
    return high, low


def phase_tables():
    lon = np.full((NY, PAD), 0)
    for q in range(NY):
        lon[q, :COLS] = q * COLS + np.arange(COLS)
    real_col = np.broadcast_to(np.arange(PAD) < COLS, (NY, PAD)).reshape(-1)
    lon = lon.reshape(-1)
    g = np.arange(KEEP_LON)
    ang = 2.0 * math.pi * ((g[:, None] * lon[None, :]) % W) / W
    fwd = np.stack([np.cos(ang), -np.sin(ang)], axis=1) * real_col / math.sqrt(W)
    fwd = fwd.reshape(2 * KEEP_LON, NY * PAD)
    gx = np.arange(KEEP_LON).reshape(NZ, NX, MODES).transpose(1, 0, 2).reshape(-1)
    ang = 2.0 * math.pi * ((lon[:, None] * gx[None, :]) % W) / W
    weight = np.where(gx == 0, 1.0, 2.0) / math.sqrt(W)
    inv = np.stack([np.cos(ang) * weight, -np.sin(ang) * weight], axis=2) * real_col[:, None, None]
    inv = inv.reshape(NY * PAD, 2 * KEEP_LON)
    lat = np.arange(H).reshape(NZ, NX, RS).transpose(1, 2, 0).reshape(-1)
    f = np.concatenate([np.arange(KEEP_LAT), np.arange(-KEEP_LAT, 0)])
    ang = 2.0 * math.pi * ((f[:, None] * lat[None, :]) % H) / H
    c, s = np.cos(ang) / math.sqrt(H), np.sin(ang) / math.sqrt(H)
    lat_fwd = np.concatenate([np.concatenate([c, s], 1), np.concatenate([-s, c], 1)], 0)
    c, s = c.T, s.T
    lat_inv = np.concatenate([np.concatenate([c, -s], 1), np.concatenate([s, c], 1)], 0)
    wide = np.stack([*split(fwd), *split(lat_fwd)])
    tall = np.stack([*split(lat_inv), *split(inv)])
    return wide, tall


def dot(a, b):
    return jnp.dot(a, b, preferred_element_type=F32)


def halves(value):
    high = value.astype(BF)
    return high, (value - high.astype(F32)).astype(BF)


def complex_weight(w_ref, k):
    re, im = w_ref[0, k], w_ref[1, k]
    return jnp.concatenate(
        [jnp.concatenate([re, im], axis=1), jnp.concatenate([-im, re], axis=1)], axis=0
    )


def kernel(
    p_hbm, w_hbm, eb_ref, gain_ref, shift_ref, w1_hbm, b1_ref, w2_hbm, b2_ref, latc, lonc, wide_hbm, tall_hbm,
    out_hbm,
    pbuf, xb, ez, wbuf, w1_ref, w2_ref, wide, tall, zs, zr, st, sb, zr1, xr1, rel, xs2, xr2, fr, ob, flat,
    w1h, w1l, w2h, w2l,
    pat_sem, wgt_sem, tab_sem, send_sem, y_sem, st_sem, z1_sem, x1_sem, x2_sem, z2_sem, out_sem,
):
    space = lax.axis_index("space")
    yi = lax.axis_index("feat")
    zi, xi = space // NX, lax.rem(space, NX)
    y_peer = lambda d: lax.rem(yi + d, NY)
    z_peer = lambda d: lax.rem(zi + d, NZ)
    x_peer = lambda d: lax.rem(xi + d, NX)
    y_id = lambda y: {"feat": y}
    z_id = lambda z: {"space": z * NX + xi}
    x_id = lambda x: {"space": zi * NX + x}
    Y_ORDER, X_ORDER, Z_ORDER = (2, 1, 3), (2, 1, 3), (4, 3, 5, 2, 6, 1, 7)

    def remote(src, dst, sends, recv, where):
        pltpu.make_async_remote_copy(
            src_ref=src, dst_ref=dst, send_sem=send_sem.at[sends], recv_sem=recv, device_id=where, device_id_type=MESH
        ).start()

    def patch_copies(r):
        for c in range(PARTS):
            pltpu.make_async_copy(p_hbm.at[r, :, c], pbuf.at[r, c], pat_sem.at[r]).start()

    patch_copies(0)
    weight_copy = pltpu.make_async_copy(w_hbm, wbuf, wgt_sem)
    weight_copy.start()

    barrier = pltpu.get_barrier_semaphore()
    for d in Y_ORDER:
        pl.semaphore_signal(barrier, inc=1, device_id=y_id(y_peer(d)), device_id_type=MESH)
    for d in Z_ORDER:
        pl.semaphore_signal(barrier, inc=1, device_id=z_id(z_peer(d)), device_id_type=MESH)
    for d in X_ORDER:
        pl.semaphore_signal(barrier, inc=1, device_id=x_id(x_peer(d)), device_id_type=MESH)

    @pl.loop(1, RS)
    def _(r):
        patch_copies(r)

    wide_copy = pltpu.make_async_copy(wide_hbm, wide, tab_sem.at[0])
    tall_copy = pltpu.make_async_copy(tall_hbm, tall, tab_sem.at[1])
    w1_copy = pltpu.make_async_copy(w1_hbm, w1_ref, tab_sem.at[2])
    w2_copy = pltpu.make_async_copy(w2_hbm, w2_ref, tab_sem.at[3])
    wide_copy.start()
    tall_copy.start()
    w1_copy.start()
    w2_copy.start()

    @pl.loop(0, ROWS)
    def _(r):
        for q in range(NY):
            zs[r, q, 80:, :] = jnp.zeros((PAD - 80, CH), BF)
        zr[r, yi, 80:, :] = jnp.zeros((PAD - 80, CH), BF)

    st[yi] = jnp.zeros((PAD, 128), F32)
    lane = lax.broadcasted_iota(jnp.int32, (PAD, 128), 1)
    channels = pl.ds(pl.multiple_of(yi * CH, CH), CH)

    weight_copy.wait()

    def embed(r):
        pltpu.make_async_copy(pbuf.at[r], pbuf.at[r], pat_sem.at[r]).wait()
        for c in range(PARTS):
            xb[:, c * LANES : (c + 1) * LANES] = pbuf[r, c].reshape(2 * COLS, LANES)
        e = dot(xb[...], wbuf[...]) + eb_ref[...]
        mean = jnp.mean(e, axis=1, keepdims=True)
        e = e - mean
        var = jnp.mean(e * e, axis=1, keepdims=True) + EPSILON
        inv = lax.rsqrt(var)
        z = e * inv
        for c in range(D // LANES):
            ez[c] = z[:, c * LANES : (c + 1) * LANES]
        at = lax.broadcasted_iota(jnp.int32, (2 * COLS, LANES), 1)
        ez[D // LANES] = jnp.where(at == 0, var * inv, mean)
        for s in range(SAMPLES):
            row = s * RS + r
            for c in range(D // LANES):
                q, half = c // 2, c % 2
                zs[row, q, 0:COLS, half * LANES : (half + 1) * LANES] = ez[c, pl.ds(s, COLS, stride=2), :].astype(BF)
            zr[row, yi] = zs[row, yi]
            stat = ez[D // LANES, pl.ds(s, COLS, stride=2), :]
            std, mean_s = stat[:, 0:1], stat[:, 1:2]
            part = lane[0:COLS]
            old = st[yi, 0:COLS]
            st[yi, 0:COLS] = jnp.where(part == 2 * row, std, jnp.where(part == 2 * row + 1, mean_s, old))

    def send_tokens(r):
        for d in Y_ORDER:
            remote(zs.at[r, y_peer(d)], zr.at[r, yi], 0, y_sem.at[r], y_id(y_peer(d)))

    embed(0)
    wide_copy.wait()
    pl.semaphore_wait(barrier, len(Y_ORDER) + len(Z_ORDER) + len(X_ORDER))

    def to_modes(r):
        pltpu.make_async_copy(zr.at[r, 0 : NY - 1], zr.at[r, 0 : NY - 1], y_sem.at[r]).wait()
        z = zr[r].reshape(NY * PAD, CH).astype(F32)
        n = (z * gain_ref[:, channels] + shift_ref[:, channels]).astype(BF)
        s = (dot(wide[0], n) + dot(wide[1], n)).reshape(NZ * NX, 2 * MODES, CH)
        s = jnp.concatenate([s[:, :, 0:128], s[:, :, 128:256]], axis=1).astype(BF)
        sb[r] = s.reshape(NZ, NX, 16, 128)
        for d in Z_ORDER:
            remote(sb.at[r, z_peer(d)], zr1.at[:, r, zi], 1, z1_sem.at[r], z_id(z_peer(d)))
        pltpu.make_async_copy(sb.at[r, zi], zr1.at[:, r, zi], z1_sem.at[r]).start()

    def pass_on(r):
        pltpu.make_async_copy(zr1.at[:, r], zr1.at[:, r], z1_sem.at[r]).wait()
        for d in X_ORDER:
            remote(zr1.at[x_peer(d), r], xr1.at[xi, r], 2, x1_sem.at[r], x_id(x_peer(d)))
        pltpu.make_async_copy(zr1.at[xi, r], xr1.at[xi, r], x1_sem.at[r]).start()

    def mix(s):
        rows = pl.ds(s * RS, RS)
        for i in range(RS):
            r = s * RS + i
            pltpu.make_async_copy(xr1.at[:, r], xr1.at[:, r], x1_sem.at[r]).wait()
        n = RS * NZ * 16
        for x in range(NX):
            rel[x * n : (x + 1) * n, :] = xr1[x, rows].astype(F32).reshape(n, 128)
        outs = []
        for k in range(2):
            cols = []
            for m in range(MODES):
                both = [rel[pl.ds(k * 8 + m * 2 + i, H, stride=16), :].astype(BF) for i in range(2)]
                cols.append(jnp.concatenate(both, axis=0))
            data = jnp.concatenate(cols, axis=1)
            g = dot(wide[2], data) + dot(wide[3], data)
            v = jnp.concatenate(
                [
                    jnp.concatenate([g[0:128, m * 128 : (m + 1) * 128], g[128:256, m * 128 : (m + 1) * 128]], axis=1)
                    for m in range(MODES)
                ],
                axis=0,
            )
            for first, (wh, wl, b_ref) in enumerate(((w1h, w1l, b1_ref), (w2h, w2l, b2_ref))):
                vh, vl = halves(v)
                bias = jnp.concatenate([b_ref[0, k : k + 1], b_ref[1, k : k + 1]], axis=1)
                v = dot(vh, wh[k]) + dot(vl, wh[k]) + dot(vh, wl[k]) + bias
                if first == 0:
                    v = jnp.maximum(v, 0.0)
            v = v - jnp.clip(v, -SHRINK, SHRINK)
            f = lax.broadcasted_iota(jnp.int32, (128, 1), 0)
            f = jnp.where(f < KEEP_LAT, f, 2 * KEEP_LAT - f)
            keep_lat = f < latc[k]
            cols = []
            for m in range(MODES):
                part = v[m * 128 : (m + 1) * 128]
                keep = jnp.logical_and(keep_lat, space * MODES + m < lonc[k])
                part = jnp.where(keep, part, 0.0)
                cols.append(jnp.concatenate([part[:, 0:128], part[:, 128:256]], axis=0))
            oh, ol = halves(jnp.concatenate(cols, axis=1))
            outs.append(dot(tall[0], oh) + dot(tall[1], oh) + dot(tall[0], ol))
        for k in range(2):
            for m in range(MODES):
                for i in range(2):
                    rel[pl.ds(k * 8 + m * 2 + i, H, stride=16), :] = outs[k][
                        i * H : (i + 1) * H, m * 128 : (m + 1) * 128
                    ]
        for x in range(NX):
            xs2[x, rows] = rel[x * n : (x + 1) * n, :].reshape(RS, NZ, 16, 128).astype(BF)
        for j in range(RS // STEP):
            some = pl.ds(s * RS + j * STEP, STEP)
            sem = x2_sem.at[s * (RS // STEP) + j]
            for d in X_ORDER:
                remote(xs2.at[x_peer(d), some], xr2.at[xi, some], 3, sem, x_id(x_peer(d)))
            pltpu.make_async_copy(xs2.at[xi, some], xr2.at[xi, some], sem).start()

    def send_back(j):
        some = pl.ds(j * STEP, STEP)
        pltpu.make_async_copy(xr2.at[:, some], xr2.at[:, some], x2_sem.at[j]).wait()
        for d in Z_ORDER:
            remote(xr2.at[:, some, z_peer(d)], fr.at[:, some, zi], 4, z2_sem.at[j], z_id(z_peer(d)))
        pltpu.make_async_copy(xr2.at[:, some, zi], fr.at[:, some, zi], z2_sem.at[j]).start()

    def out_copy(r):
        return pltpu.make_async_copy(ob.at[r], out_hbm.at[r], out_sem)

    def to_tokens(r):
        a = fr[:, r].astype(F32).reshape(NX * NZ, 16, 128)
        a = jnp.concatenate([a[:, 0:8], a[:, 8:16]], axis=2).reshape(2 * KEEP_LON, CH).astype(BF)
        filtered = dot(tall[2], a) + dot(tall[3], a)
        for q in range(NY):
            stat = st[q]
            std = jnp.sum(jnp.where(lane == 2 * r, stat, 0.0), axis=1, keepdims=True)
            mean = jnp.sum(jnp.where(lane == 2 * r + 1, stat, 0.0), axis=1, keepdims=True)
            mixed = filtered[q * PAD : (q + 1) * PAD] + (zr[r, q].astype(F32) * std + mean)
            flat[q * COLS : (q + 1) * COLS, :] = mixed[0:COLS]
        ob[r] = flat[...].astype(BF)
        out_copy(r).start()

    def finish(j):
        some = pl.ds(j * STEP, STEP)
        pltpu.make_async_copy(fr.at[:, some], fr.at[:, some], z2_sem.at[j]).wait()

        @pl.loop(0, STEP)
        def _(i):
            to_tokens(j * STEP + i)

    @pl.loop(0, ROWS + LAG)
    def _(i):
        @pl.when(i < ROWS)
        def _():
            send_tokens(i)

        @pl.when(i < RS - 1)
        def _():
            embed(i + 1)

        @pl.when(i == RS)
        def _():
            w1_copy.wait()
            w2_copy.wait()
            for k in range(2):
                w1h[k], w1l[k] = halves(complex_weight(w1_ref, k))
                w2h[k], w2l[k] = halves(complex_weight(w2_ref, k))

        @pl.when(i == ROWS - 1)
        def _():
            for d in Y_ORDER:
                remote(st.at[yi], st.at[yi], 5, st_sem, y_id(y_peer(d)))

        @pl.when(i >= LAG)
        def _():
            to_modes(i - LAG)

        @pl.when(i >= LAG + FWD)
        def _():
            pass_on(i - LAG - FWD)

    tall_copy.wait()
    half = RS // STEP
    mix(0)

    @pl.loop(ROWS - FWD, ROWS)
    def _(r):
        pass_on(r)

    @pl.loop(0, half)
    def _(j):
        send_back(j)

    mix(1)
    pltpu.make_async_copy(st.at[0 : NY - 1], st.at[0 : NY - 1], st_sem).wait()
    finish(0)

    @pl.loop(half, 2 * half)
    def _(j):
        send_back(j)

    @pl.loop(1, 2 * half)
    def _(j):
        finish(j)

    for sends, ref in enumerate(
        (
            zs.at[:, 0 : NY - 1],
            sb.at[:, 0 : NZ - 1],
            zr1.at[0 : NX - 1],
            xs2.at[0 : NX - 1],
            xr2.at[:, :, 0 : NZ - 1],
            st.at[0 : NY - 1],
        )
    ):
        pltpu.make_async_copy(ref, ref, send_sem.at[sends]).wait()
    pltpu.make_async_copy(ob, out_hbm, out_sem).wait()


def solution(mesh):
    wide, tall = phase_tables()

    def local(
        patches, embed_weight, embed_bias, norm_gain, norm_bias, w_one, b_one, w_two, b_two, lat_cut, lon_cut
    ):
        anywhere = pl.BlockSpec(memory_space=pltpu.HBM)
        vmem = pl.BlockSpec(memory_space=pltpu.VMEM)
        smem = pl.BlockSpec(memory_space=pltpu.SMEM)
        back = (NX, ROWS, NZ, 16, 128)
        out = pl.pallas_call(
            kernel,
            out_shape=jax.ShapeDtypeStruct((ROWS, W, CH), BF),
            in_specs=[anywhere, anywhere, vmem, vmem, vmem, anywhere, vmem, anywhere, vmem, smem, smem, anywhere, anywhere],
            out_specs=pl.BlockSpec(memory_space=pl.ANY),
            scratch_shapes=[
                pltpu.VMEM((RS, PARTS, COLS, SAMPLES, LANES), BF),
                pltpu.VMEM((2 * COLS, PATCH), BF),
                pltpu.VMEM((D // LANES + 1, 2 * COLS, LANES), F32),
                pltpu.VMEM((PATCH, D), BF),
                pltpu.VMEM((2, 2, 128, 128), F32),
                pltpu.VMEM((2, 2, 128, 128), F32),
                pltpu.VMEM((4, 256, 384), BF),
                pltpu.VMEM((4, 384, 256), BF),
                pltpu.VMEM((ROWS, NY, PAD, CH), BF),
                pltpu.VMEM((ROWS, NY, PAD, CH), BF),
                pltpu.VMEM((NY, PAD, 128), F32),
                pltpu.VMEM((ROWS, NZ, NX, 16, 128), BF),
                pltpu.VMEM(back, BF),
                pltpu.VMEM(back, BF),
                pltpu.VMEM((H * 16, 128), F32),
                pltpu.VMEM(back, BF),
                pltpu.VMEM(back, BF),
                pltpu.VMEM(back, BF),
                pltpu.VMEM((ROWS, W, CH), BF),
                pltpu.VMEM((W, CH), F32),
            ]
            + [pltpu.VMEM((2, 256, 256), BF)] * 4
            + [
                pltpu.SemaphoreType.DMA((RS,)),
                pltpu.SemaphoreType.DMA,
                pltpu.SemaphoreType.DMA((4,)),
                pltpu.SemaphoreType.DMA((6,)),
                pltpu.SemaphoreType.DMA((ROWS,)),
                pltpu.SemaphoreType.DMA,
                pltpu.SemaphoreType.DMA((ROWS,)),
                pltpu.SemaphoreType.DMA((ROWS,)),
                pltpu.SemaphoreType.DMA((ROWS // STEP,)),
                pltpu.SemaphoreType.DMA((ROWS // STEP,)),
                pltpu.SemaphoreType.DMA,
            ],
            compiler_params=pltpu.CompilerParams(
                collective_id=0, has_side_effects=True, vmem_limit_bytes=54 * 1024 * 1024
            ),
            name="afno",
        )(
            patches.reshape(SAMPLES, RS, COLS, PARTS, LANES).transpose(1, 2, 3, 0, 4),
            embed_weight,
            embed_bias.reshape(1, D),
            norm_gain.reshape(1, D),
            norm_bias.reshape(1, D),
            w_one,
            b_one,
            w_two,
            b_two,
            lat_cut,
            lon_cut,
            jnp.asarray(wide),
            jnp.asarray(tall),
        )
        return out.reshape(SAMPLES, RS, W, CH)

    in_specs = (
        P("dp", "space", "feat", None),
        P(),
        P(),
        P(),
        P(),
        P(None, "feat", None, None),
        P(None, "feat", None),
        P(None, "feat", None, None),
        P(None, "feat", None),
        P("feat"),
        P("feat"),
    )
    return jax.shard_map(
        local, mesh=mesh, in_specs=in_specs, out_specs=P("dp", "space", None, "feat"), check_vma=False
    )
```

```python
import functools
import math

import jax
import jax.numpy as jnp
import ml_dtypes
import numpy as np
from jax import lax
from jax.experimental import pallas as pl
from jax.experimental.pallas import tpu as pltpu
from jax.sharding import PartitionSpec as P

MESH = pl.DeviceIdType.MESH
BF = jnp.bfloat16
F32 = jnp.float32

SAMPLES, H, W = 2, 192, 360
PATCH, D = 1280, 1024
KEEP_LAT, KEEP_LON = 64, 128
SHRINK = 0.01
EPSILON = 1e-05

NZ, NX, NY = 8, 4, 4
RS = H // (NZ * NX)
ROWS = SAMPLES * RS
COLS = W // NY
PAD = 96
CH = D // NY
MODES = KEEP_LON // (NZ * NX)
LANES = 128
PARTS = PATCH // LANES
LAG = 2
FWD = 4
OUT_GROUPS = ((0, 1), (1, 2), (2, 4), (4, 6), (6, 8), (8, 10), (10, 11), (11, 12))
BACK_GROUPS = ((0, 1), (1, 3), (3, 6), (6, 7), (7, 9), (9, 11), (11, 12))


def split(table):
    high = table.astype(ml_dtypes.bfloat16)
    low = (table - high.astype(np.float64)).astype(ml_dtypes.bfloat16)
    return high, low


def phase_tables():
    lon = np.full((NY, PAD), 0)
    for q in range(NY):
        lon[q, :COLS] = q * COLS + np.arange(COLS)
    real_col = np.broadcast_to(np.arange(PAD) < COLS, (NY, PAD)).reshape(-1)
    lon = lon.reshape(-1)
    g = np.arange(KEEP_LON)
    ang = 2.0 * math.pi * ((g[:, None] * lon[None, :]) % W) / W
    fwd = np.stack([np.cos(ang), -np.sin(ang)], axis=1) * real_col / math.sqrt(W)
    fwd = fwd.reshape(2 * KEEP_LON, NY * PAD)
    gx = np.arange(KEEP_LON).reshape(NZ, NX, MODES).transpose(1, 0, 2).reshape(-1)
    ang = 2.0 * math.pi * ((lon[:, None] * gx[None, :]) % W) / W
    weight = np.where(gx == 0, 1.0, 2.0) / math.sqrt(W)
    inv = np.stack([np.cos(ang) * weight, -np.sin(ang) * weight], axis=2) * real_col[:, None, None]
    inv = inv.reshape(NY * PAD, 2 * KEEP_LON)
    lat = np.arange(H).reshape(NZ, NX, RS).transpose(1, 2, 0).reshape(-1)
    f = np.concatenate([np.arange(KEEP_LAT), np.arange(-KEEP_LAT, 0)])
    ang = 2.0 * math.pi * ((f[:, None] * lat[None, :]) % H) / H
    c, s = np.cos(ang) / math.sqrt(H), np.sin(ang) / math.sqrt(H)
    lat_fwd = np.concatenate([np.concatenate([c, s], 1), np.concatenate([-s, c], 1)], 0)
    c, s = c.T, s.T
    lat_inv = np.concatenate([np.concatenate([c, -s], 1), np.concatenate([s, c], 1)], 0)
    wide = np.stack([*split(fwd), *split(lat_fwd)])
    tall = np.stack([*split(lat_inv), *split(inv)])
    return wide, tall


def dot(a, b):
    return jnp.dot(a, b, preferred_element_type=F32)


def halves(value):
    high = value.astype(BF)
    return high, (value - high.astype(F32)).astype(BF)


def complex_weight(w_ref, k):
    re, im = w_ref[0, k], w_ref[1, k]
    return jnp.concatenate(
        [jnp.concatenate([re, im], axis=1), jnp.concatenate([-im, re], axis=1)], axis=0
    )


def kernel(
    p_hbm, w_hbm, eb_ref, gain_ref, shift_ref, w1_hbm, b1_ref, w2_hbm, b2_ref, latc, lonc, wide_hbm, tall_hbm,
    out_hbm,
    pbuf, xb, ez, wbuf, w1_ref, w2_ref, wide, tall, zs, zr, st, sb, zr1, xr1, rel, xs2, xr2, fr, ob, flat,
    w1h, w1l, w2h, w2l,
    pat_sem, wgt_sem, tab_sem, send_sem, y_sem, st_sem, z1_sem, x1_sem, x2_sem, z2_sem, out_sem,
):
    space = lax.axis_index("space")
    yi = lax.axis_index("feat")
    zi, xi = space // NX, lax.rem(space, NX)
    y_peer = lambda d: lax.rem(yi + d, NY)
    z_peer = lambda d: lax.rem(zi + d, NZ)
    x_peer = lambda d: lax.rem(xi + d, NX)
    y_id = lambda y: {"feat": y}
    z_id = lambda z: {"space": z * NX + xi}
    x_id = lambda x: {"space": zi * NX + x}
    Y_ORDER, X_ORDER, Z_ORDER = (2, 1, 3), (2, 1, 3), (4, 3, 5, 2, 6, 1, 7)

    def remote(src, dst, sends, recv, where):
        pltpu.make_async_remote_copy(
            src_ref=src, dst_ref=dst, send_sem=send_sem.at[sends], recv_sem=recv, device_id=where, device_id_type=MESH
        ).start()

    def patch_copies(r):
        for c in range(PARTS):
            pltpu.make_async_copy(p_hbm.at[r, :, c], pbuf.at[r, c], pat_sem.at[r]).start()

    patch_copies(0)
    weight_copy = pltpu.make_async_copy(w_hbm, wbuf, wgt_sem)
    weight_copy.start()

    barrier = pltpu.get_barrier_semaphore()
    for d in Y_ORDER:
        pl.semaphore_signal(barrier, inc=1, device_id=y_id(y_peer(d)), device_id_type=MESH)
    for d in Z_ORDER:
        pl.semaphore_signal(barrier, inc=1, device_id=z_id(z_peer(d)), device_id_type=MESH)
    for d in X_ORDER:
        pl.semaphore_signal(barrier, inc=1, device_id=x_id(x_peer(d)), device_id_type=MESH)

    @pl.loop(1, RS)
    def _(r):
        patch_copies(r)

    wide_copy = pltpu.make_async_copy(wide_hbm, wide, tab_sem.at[0])
    tall_copy = pltpu.make_async_copy(tall_hbm, tall, tab_sem.at[1])
    w1_copy = pltpu.make_async_copy(w1_hbm, w1_ref, tab_sem.at[2])
    w2_copy = pltpu.make_async_copy(w2_hbm, w2_ref, tab_sem.at[3])
    wide_copy.start()
    tall_copy.start()
    w1_copy.start()
    w2_copy.start()

    @pl.loop(0, ROWS)
    def _(r):
        for q in range(NY):
            zs[r, q, 80:, :] = jnp.zeros((PAD - 80, CH), BF)
        zr[r, yi, 80:, :] = jnp.zeros((PAD - 80, CH), BF)

    st[yi] = jnp.zeros((PAD, 128), F32)
    lane = lax.broadcasted_iota(jnp.int32, (PAD, 128), 1)
    channels = pl.ds(pl.multiple_of(yi * CH, CH), CH)

    weight_copy.wait()

    def embed(r):
        pltpu.make_async_copy(pbuf.at[r], pbuf.at[r], pat_sem.at[r]).wait()
        for c in range(PARTS):
            xb[:, c * LANES : (c + 1) * LANES] = pbuf[r, c].reshape(2 * COLS, LANES)
        e = dot(xb[...], wbuf[...]) + eb_ref[...]
        mean = jnp.mean(e, axis=1, keepdims=True)
        e = e - mean
        var = jnp.mean(e * e, axis=1, keepdims=True) + EPSILON
        inv = lax.rsqrt(var)
        z = e * inv
        for c in range(D // LANES):
            ez[c] = z[:, c * LANES : (c + 1) * LANES]
        at = lax.broadcasted_iota(jnp.int32, (2 * COLS, LANES), 1)
        ez[D // LANES] = jnp.where(at == 0, var * inv, mean)
        for s in range(SAMPLES):
            row = s * RS + r
            for c in range(D // LANES):
                q, half = c // 2, c % 2
                zs[row, q, 0:COLS, half * LANES : (half + 1) * LANES] = ez[c, pl.ds(s, COLS, stride=2), :].astype(BF)
            zr[row, yi] = zs[row, yi]
            stat = ez[D // LANES, pl.ds(s, COLS, stride=2), :]
            std, mean_s = stat[:, 0:1], stat[:, 1:2]
            part = lane[0:COLS]
            old = st[yi, 0:COLS]
            st[yi, 0:COLS] = jnp.where(part == 2 * row, std, jnp.where(part == 2 * row + 1, mean_s, old))

    def send_tokens(r):
        for d in Y_ORDER:
            remote(zs.at[r, y_peer(d)], zr.at[r, yi], 0, y_sem.at[r], y_id(y_peer(d)))

    embed(0)
    wide_copy.wait()
    pl.semaphore_wait(barrier, len(Y_ORDER) + len(Z_ORDER) + len(X_ORDER))

    def to_modes(r):
        pltpu.make_async_copy(zr.at[r, 0 : NY - 1], zr.at[r, 0 : NY - 1], y_sem.at[r]).wait()
        z = zr[r].reshape(NY * PAD, CH).astype(F32)
        n = (z * gain_ref[:, channels] + shift_ref[:, channels]).astype(BF)
        s = (dot(wide[0], n) + dot(wide[1], n)).reshape(NZ * NX, 2 * MODES, CH)
        s = jnp.concatenate([s[:, :, 0:128], s[:, :, 128:256]], axis=1).astype(BF)
        s = s.reshape(NZ, NX, 16, 128)
        for x in range(NX):
            sb[x, r] = s[:, x]

    def some_rows(groups, g):
        return pl.ds(groups[g][0], groups[g][1] - groups[g][0])

    def send_modes(g):
        rows = some_rows(OUT_GROUPS, g)
        for d in Z_ORDER:
            remote(sb.at[:, rows, z_peer(d)], zr1.at[:, rows, zi], 1, z1_sem.at[g], z_id(z_peer(d)))
        pltpu.make_async_copy(sb.at[:, rows, zi], zr1.at[:, rows, zi], z1_sem.at[g]).start()

    def pass_on(g):
        rows = some_rows(OUT_GROUPS, g)
        pltpu.make_async_copy(zr1.at[:, rows], zr1.at[:, rows], z1_sem.at[g]).wait()
        for d in X_ORDER:
            remote(zr1.at[x_peer(d), rows], xr1.at[xi, rows], 2, x1_sem.at[g], x_id(x_peer(d)))
        pltpu.make_async_copy(zr1.at[xi, rows], xr1.at[xi, rows], x1_sem.at[g]).start()

    def mix(s):
        rows = pl.ds(s * RS, RS)
        for g, (low, _) in enumerate(OUT_GROUPS):
            if low // RS == s:
                some = some_rows(OUT_GROUPS, g)
                pltpu.make_async_copy(xr1.at[:, some], xr1.at[:, some], x1_sem.at[g]).wait()
        n = RS * NZ * 16
        for x in range(NX):
            rel[x * n : (x + 1) * n, :] = xr1[x, rows].astype(F32).reshape(n, 128)
        outs = []
        for k in range(2):
            cols = []
            for m in range(MODES):
                both = [rel[pl.ds(k * 8 + m * 2 + i, H, stride=16), :].astype(BF) for i in range(2)]
                cols.append(jnp.concatenate(both, axis=0))
            data = jnp.concatenate(cols, axis=1)
            g = dot(wide[2], data) + dot(wide[3], data)
            v = jnp.concatenate(
                [
                    jnp.concatenate([g[0:128, m * 128 : (m + 1) * 128], g[128:256, m * 128 : (m + 1) * 128]], axis=1)
                    for m in range(MODES)
                ],
                axis=0,
            )
            for first, (wh, wl, b_ref) in enumerate(((w1h, w1l, b1_ref), (w2h, w2l, b2_ref))):
                vh, vl = halves(v)
                bias = jnp.concatenate([b_ref[0, k : k + 1], b_ref[1, k : k + 1]], axis=1)
                v = dot(vh, wh[k]) + dot(vl, wh[k]) + dot(vh, wl[k]) + bias
                if first == 0:
                    v = jnp.maximum(v, 0.0)
            v = v - jnp.clip(v, -SHRINK, SHRINK)
            f = lax.broadcasted_iota(jnp.int32, (128, 1), 0)
            f = jnp.where(f < KEEP_LAT, f, 2 * KEEP_LAT - f)
            keep_lat = f < latc[k]
            cols = []
            for m in range(MODES):
                part = v[m * 128 : (m + 1) * 128]
                keep = jnp.logical_and(keep_lat, space * MODES + m < lonc[k])
                part = jnp.where(keep, part, 0.0)
                cols.append(jnp.concatenate([part[:, 0:128], part[:, 128:256]], axis=0))
            oh, ol = halves(jnp.concatenate(cols, axis=1))
            outs.append(dot(tall[0], oh) + dot(tall[1], oh) + dot(tall[0], ol))
        for k in range(2):
            for m in range(MODES):
                for i in range(2):
                    rel[pl.ds(k * 8 + m * 2 + i, H, stride=16), :] = outs[k][
                        i * H : (i + 1) * H, m * 128 : (m + 1) * 128
                    ]
        for x in range(NX):
            xs2[x, rows] = rel[x * n : (x + 1) * n, :].reshape(RS, NZ, 16, 128).astype(BF)
        for j, (low, _) in enumerate(BACK_GROUPS):
            if low // RS == s:
                some = some_rows(BACK_GROUPS, j)
                for d in X_ORDER:
                    remote(xs2.at[x_peer(d), some], xr2.at[xi, some], 3, x2_sem.at[j], x_id(x_peer(d)))
                pltpu.make_async_copy(xs2.at[xi, some], xr2.at[xi, some], x2_sem.at[j]).start()

    def send_back(j):
        some = some_rows(BACK_GROUPS, j)
        pltpu.make_async_copy(xr2.at[:, some], xr2.at[:, some], x2_sem.at[j]).wait()
        for d in Z_ORDER:
            remote(xr2.at[:, some, z_peer(d)], fr.at[:, some, zi], 4, z2_sem.at[j], z_id(z_peer(d)))
        pltpu.make_async_copy(xr2.at[:, some, zi], fr.at[:, some, zi], z2_sem.at[j]).start()

    def out_copy(r):
        return pltpu.make_async_copy(ob.at[r], out_hbm.at[r], out_sem)

    def to_tokens(r):
        a = fr[:, r].astype(F32).reshape(NX * NZ, 16, 128)
        a = jnp.concatenate([a[:, 0:8], a[:, 8:16]], axis=2).reshape(2 * KEEP_LON, CH).astype(BF)
        filtered = dot(tall[2], a) + dot(tall[3], a)
        for q in range(NY):
            stat = st[q]
            std = jnp.sum(jnp.where(lane == 2 * r, stat, 0.0), axis=1, keepdims=True)
            mean = jnp.sum(jnp.where(lane == 2 * r + 1, stat, 0.0), axis=1, keepdims=True)
            mixed = filtered[q * PAD : (q + 1) * PAD] + (zr[r, q].astype(F32) * std + mean)
            flat[q * COLS : (q + 1) * COLS, :] = mixed[0:COLS]
        ob[r] = flat[...].astype(BF)
        out_copy(r).start()

    @pl.loop(0, ROWS + LAG)
    def _(i):
        @pl.when(i < ROWS)
        def _():
            send_tokens(i)

        @pl.when(i < RS - 1)
        def _():
            embed(i + 1)

        @pl.when(i == RS)
        def _():
            w1_copy.wait()
            w2_copy.wait()
            for k in range(2):
                w1h[k], w1l[k] = halves(complex_weight(w1_ref, k))
                w2h[k], w2l[k] = halves(complex_weight(w2_ref, k))

        @pl.when(i == ROWS - 1)
        def _():
            for d in Y_ORDER:
                remote(st.at[yi], st.at[yi], 5, st_sem, y_id(y_peer(d)))

        @pl.when(i >= LAG)
        def _():
            to_modes(i - LAG)

        for g, (_, high) in enumerate(OUT_GROUPS):
            pl.when(i == LAG + high - 1)(functools.partial(send_modes, g))
            if high + FWD <= ROWS:
                pl.when(i == LAG + high - 1 + FWD)(functools.partial(pass_on, g))

    tall_copy.wait()
    mix(0)
    pass_on(5)
    send_back(0)
    send_back(1)
    pass_on(6)
    send_back(2)
    pass_on(7)
    mix(1)
    send_back(3)
    pltpu.make_async_copy(st.at[0 : NY - 1], st.at[0 : NY - 1], st_sem).wait()

    @pl.loop(0, ROWS)
    def _(r):
        for j, (low, _) in enumerate(BACK_GROUPS):

            @pl.when(r == low)
            def _(j=j):
                some = some_rows(BACK_GROUPS, j)
                pltpu.make_async_copy(fr.at[:, some], fr.at[:, some], z2_sem.at[j]).wait()

        to_tokens(r)
        for j in range(4, len(BACK_GROUPS)):
            pl.when(r == j - 4)(functools.partial(send_back, j))

    for sends, ref in enumerate(
        (
            zs.at[:, 0 : NY - 1],
            sb.at[:, :, 0 : NZ - 1],
            zr1.at[0 : NX - 1],
            xs2.at[0 : NX - 1],
            xr2.at[:, :, 0 : NZ - 1],
            st.at[0 : NY - 1],
        )
    ):
        pltpu.make_async_copy(ref, ref, send_sem.at[sends]).wait()
    pltpu.make_async_copy(ob, out_hbm, out_sem).wait()


def copy_rows(src, dst, held, in_sem, out_sem):
    for r in range(ROWS):
        pltpu.make_async_copy(src.at[r], held.at[r], in_sem.at[r]).start()
    for r in range(ROWS):
        pltpu.make_async_copy(src.at[r], held.at[r], in_sem.at[r]).wait()
        pltpu.make_async_copy(held.at[r], dst.at[r], out_sem.at[r]).start()
    for r in range(ROWS):
        pltpu.make_async_copy(held.at[r], dst.at[r], out_sem.at[r]).wait()


def solution(mesh):
    wide, tall = phase_tables()

    def local(
        patches, embed_weight, embed_bias, norm_gain, norm_bias, w_one, b_one, w_two, b_two, lat_cut, lon_cut
    ):
        anywhere = pl.BlockSpec(memory_space=pltpu.HBM)
        vmem = pl.BlockSpec(memory_space=pltpu.VMEM)
        smem = pl.BlockSpec(memory_space=pltpu.SMEM)
        back = (NX, ROWS, NZ, 16, 128)
        out = pl.pallas_call(
            kernel,
            out_shape=jax.ShapeDtypeStruct((ROWS, W, CH), BF),
            in_specs=[anywhere, anywhere, vmem, vmem, vmem, anywhere, vmem, anywhere, vmem, smem, smem, anywhere, anywhere],
            out_specs=pl.BlockSpec(memory_space=pl.ANY),
            scratch_shapes=[
                pltpu.VMEM((RS, PARTS, COLS, SAMPLES, LANES), BF),
                pltpu.VMEM((2 * COLS, PATCH), BF),
                pltpu.VMEM((D // LANES + 1, 2 * COLS, LANES), F32),
                pltpu.VMEM((PATCH, D), BF),
                pltpu.VMEM((2, 2, 128, 128), F32),
                pltpu.VMEM((2, 2, 128, 128), F32),
                pltpu.VMEM((4, 256, 384), BF),
                pltpu.VMEM((4, 384, 256), BF),
                pltpu.VMEM((ROWS, NY, PAD, CH), BF),
                pltpu.VMEM((ROWS, NY, PAD, CH), BF),
                pltpu.VMEM((NY, PAD, 128), F32),
                pltpu.VMEM(back, BF),
                pltpu.VMEM(back, BF),
                pltpu.VMEM(back, BF),
                pltpu.VMEM((H * 16, 128), F32),
                pltpu.VMEM(back, BF),
                pltpu.VMEM(back, BF),
                pltpu.VMEM(back, BF),
                pltpu.VMEM((ROWS, W, CH), BF),
                pltpu.VMEM((W, CH), F32),
            ]
            + [pltpu.VMEM((2, 256, 256), BF)] * 4
            + [
                pltpu.SemaphoreType.DMA((RS,)),
                pltpu.SemaphoreType.DMA,
                pltpu.SemaphoreType.DMA((4,)),
                pltpu.SemaphoreType.DMA((6,)),
                pltpu.SemaphoreType.DMA((ROWS,)),
                pltpu.SemaphoreType.DMA,
                pltpu.SemaphoreType.DMA((len(OUT_GROUPS),)),
                pltpu.SemaphoreType.DMA((len(OUT_GROUPS),)),
                pltpu.SemaphoreType.DMA((len(BACK_GROUPS),)),
                pltpu.SemaphoreType.DMA((len(BACK_GROUPS),)),
                pltpu.SemaphoreType.DMA,
            ],
            compiler_params=pltpu.CompilerParams(
                collective_id=0, has_side_effects=True, vmem_limit_bytes=54 * 1024 * 1024
            ),
            name="afno",
        )(
            patches.reshape(SAMPLES, RS, COLS, PARTS, LANES).transpose(1, 2, 3, 0, 4),
            embed_weight,
            embed_bias.reshape(1, D),
            norm_gain.reshape(1, D),
            norm_bias.reshape(1, D),
            w_one,
            b_one,
            w_two,
            b_two,
            lat_cut,
            lon_cut,
            jnp.asarray(wide),
            jnp.asarray(tall),
        )
        out = pl.pallas_call(
            copy_rows,
            out_shape=jax.ShapeDtypeStruct((ROWS, W, CH), BF),
            in_specs=[anywhere],
            out_specs=pl.BlockSpec(memory_space=pl.ANY),
            scratch_shapes=[
                pltpu.VMEM((ROWS, W, CH), BF),
                pltpu.SemaphoreType.DMA((ROWS,)),
                pltpu.SemaphoreType.DMA((ROWS,)),
            ],
            name="copy_rows",
        )(out)
        return out.reshape(SAMPLES, RS, W, CH)

    in_specs = (
        P("dp", "space", "feat", None),
        P(),
        P(),
        P(),
        P(),
        P(None, "feat", None, None),
        P(None, "feat", None),
        P(None, "feat", None, None),
        P(None, "feat", None),
        P("feat"),
        P("feat"),
    )
    return jax.shard_map(
        local, mesh=mesh, in_specs=in_specs, out_specs=P("dp", "space", None, "feat"), check_vma=False
    )
```

```python
import functools
import math

import jax
import jax.numpy as jnp
import ml_dtypes
import numpy as np
from jax import lax
from jax.experimental import pallas as pl
from jax.experimental.pallas import tpu as pltpu
from jax.sharding import PartitionSpec as P

MESH = pl.DeviceIdType.MESH
BF = jnp.bfloat16
F32 = jnp.float32

SAMPLES, H, W = 2, 192, 360
PATCH, D = 1280, 1024
KEEP_LAT, KEEP_LON = 64, 128
SHRINK = 0.01
EPSILON = 1e-05

NZ, NX, NY = 8, 4, 4
RS = H // (NZ * NX)
ROWS = SAMPLES * RS
COLS = W // NY
PAD = 96
CH = D // NY
MODES = KEEP_LON // (NZ * NX)
LANES = 128
PARTS = PATCH // LANES
LAG = 2
FWD = 4
OUT_GROUPS = ((0, 1), (1, 2), (2, 4), (4, 6), (6, 8), (8, 10), (10, 11), (11, 12))
COPY = 3
BACK_GROUPS = ((0, 1), (1, 3), (3, 6), (6, 7), (7, 9), (9, 11), (11, 12))


def split(table):
    high = table.astype(ml_dtypes.bfloat16)
    low = (table - high.astype(np.float64)).astype(ml_dtypes.bfloat16)
    return high, low


def phase_tables():
    lon = np.full((NY, PAD), 0)
    for q in range(NY):
        lon[q, :COLS] = q * COLS + np.arange(COLS)
    real_col = np.broadcast_to(np.arange(PAD) < COLS, (NY, PAD)).reshape(-1)
    lon = lon.reshape(-1)
    g = np.arange(KEEP_LON)
    ang = 2.0 * math.pi * ((g[:, None] * lon[None, :]) % W) / W
    fwd = np.stack([np.cos(ang), -np.sin(ang)], axis=1) * real_col / math.sqrt(W)
    fwd = fwd.reshape(2 * KEEP_LON, NY * PAD)
    gx = np.arange(KEEP_LON).reshape(NZ, NX, MODES).transpose(1, 0, 2).reshape(-1)
    ang = 2.0 * math.pi * ((lon[:, None] * gx[None, :]) % W) / W
    weight = np.where(gx == 0, 1.0, 2.0) / math.sqrt(W)
    inv = np.stack([np.cos(ang) * weight, -np.sin(ang) * weight], axis=2) * real_col[:, None, None]
    inv = inv.reshape(NY * PAD, 2 * KEEP_LON)
    lat = np.arange(H).reshape(NZ, NX, RS).transpose(1, 2, 0).reshape(-1)
    f = np.concatenate([np.arange(KEEP_LAT), np.arange(-KEEP_LAT, 0)])
    ang = 2.0 * math.pi * ((f[:, None] * lat[None, :]) % H) / H
    c, s = np.cos(ang) / math.sqrt(H), np.sin(ang) / math.sqrt(H)
    lat_fwd = np.concatenate([np.concatenate([c, s], 1), np.concatenate([-s, c], 1)], 0)
    c, s = c.T, s.T
    lat_inv = np.concatenate([np.concatenate([c, -s], 1), np.concatenate([s, c], 1)], 0)
    wide = np.stack([*split(fwd), *split(lat_fwd)])
    tall = np.stack([*split(lat_inv), *split(inv)])
    return wide, tall


def dot(a, b):
    return jnp.dot(a, b, preferred_element_type=F32)


def halves(value):
    high = value.astype(BF)
    return high, (value - high.astype(F32)).astype(BF)


def complex_weight(w_ref, k):
    re, im = w_ref[0, k], w_ref[1, k]
    return jnp.concatenate(
        [jnp.concatenate([re, im], axis=1), jnp.concatenate([-im, re], axis=1)], axis=0
    )


def kernel(
    p_hbm, w_hbm, eb_ref, gain_ref, shift_ref, w1_hbm, b1_ref, w2_hbm, b2_ref, latc, lonc, wide_hbm, tall_hbm,
    out_hbm,
    pbuf, xb, ez, wbuf, w1_ref, w2_ref, wide, tall, zs, zr, st, sb, zr1, xr1, rel, xs2, xr2, fr, ob, flat,
    w1h, w1l, w2h, w2l,
    pat_sem, wgt_sem, tab_sem, send_sem, y_sem, st_sem, z1_sem, x1_sem, x2_sem, z2_sem, out_sem,
):
    space = lax.axis_index("space")
    yi = lax.axis_index("feat")
    zi, xi = space // NX, lax.rem(space, NX)
    y_peer = lambda d: lax.rem(yi + d, NY)
    z_peer = lambda d: lax.rem(zi + d, NZ)
    x_peer = lambda d: lax.rem(xi + d, NX)
    y_id = lambda y: {"feat": y}
    z_id = lambda z: {"space": z * NX + xi}
    x_id = lambda x: {"space": zi * NX + x}
    Y_ORDER, X_ORDER, Z_ORDER = (2, 1, 3), (2, 1, 3), (4, 3, 5, 2, 6, 1, 7)

    def remote(src, dst, sends, recv, where):
        pltpu.make_async_remote_copy(
            src_ref=src, dst_ref=dst, send_sem=send_sem.at[sends], recv_sem=recv, device_id=where, device_id_type=MESH
        ).start()

    def patch_copies(r):
        for c in range(PARTS):
            pltpu.make_async_copy(p_hbm.at[r, :, c], pbuf.at[r, c], pat_sem.at[r]).start()

    patch_copies(0)
    weight_copy = pltpu.make_async_copy(w_hbm, wbuf, wgt_sem)
    weight_copy.start()

    barrier = pltpu.get_barrier_semaphore()
    for d in Y_ORDER:
        pl.semaphore_signal(barrier, inc=1, device_id=y_id(y_peer(d)), device_id_type=MESH)
    for d in Z_ORDER:
        pl.semaphore_signal(barrier, inc=1, device_id=z_id(z_peer(d)), device_id_type=MESH)
    for d in X_ORDER:
        pl.semaphore_signal(barrier, inc=1, device_id=x_id(x_peer(d)), device_id_type=MESH)

    @pl.loop(1, RS)
    def _(r):
        patch_copies(r)

    wide_copy = pltpu.make_async_copy(wide_hbm, wide, tab_sem.at[0])
    tall_copy = pltpu.make_async_copy(tall_hbm, tall, tab_sem.at[1])
    w1_copy = pltpu.make_async_copy(w1_hbm, w1_ref, tab_sem.at[2])
    w2_copy = pltpu.make_async_copy(w2_hbm, w2_ref, tab_sem.at[3])
    wide_copy.start()
    tall_copy.start()
    w1_copy.start()
    w2_copy.start()

    @pl.loop(0, ROWS)
    def _(r):
        for q in range(NY):
            zs[r, q, 80:, :] = jnp.zeros((PAD - 80, CH), BF)
        zr[r, yi, 80:, :] = jnp.zeros((PAD - 80, CH), BF)

    st[yi] = jnp.zeros((PAD, 128), F32)
    lane = lax.broadcasted_iota(jnp.int32, (PAD, 128), 1)
    channels = pl.ds(pl.multiple_of(yi * CH, CH), CH)

    weight_copy.wait()

    def embed(r):
        pltpu.make_async_copy(pbuf.at[r], pbuf.at[r], pat_sem.at[r]).wait()
        for c in range(PARTS):
            xb[:, c * LANES : (c + 1) * LANES] = pbuf[r, c].reshape(2 * COLS, LANES)
        e = dot(xb[...], wbuf[...]) + eb_ref[...]
        mean = jnp.mean(e, axis=1, keepdims=True)
        e = e - mean
        var = jnp.mean(e * e, axis=1, keepdims=True) + EPSILON
        inv = lax.rsqrt(var)
        z = e * inv
        for c in range(D // LANES):
            ez[c] = z[:, c * LANES : (c + 1) * LANES]
        at = lax.broadcasted_iota(jnp.int32, (2 * COLS, LANES), 1)
        ez[D // LANES] = jnp.where(at == 0, var * inv, mean)
        for s in range(SAMPLES):
            row = s * RS + r
            for c in range(D // LANES):
                q, half = c // 2, c % 2
                zs[row, q, 0:COLS, half * LANES : (half + 1) * LANES] = ez[c, pl.ds(s, COLS, stride=2), :].astype(BF)
            zr[row, yi] = zs[row, yi]
            stat = ez[D // LANES, pl.ds(s, COLS, stride=2), :]
            std, mean_s = stat[:, 0:1], stat[:, 1:2]
            part = lane[0:COLS]
            old = st[yi, 0:COLS]
            st[yi, 0:COLS] = jnp.where(part == 2 * row, std, jnp.where(part == 2 * row + 1, mean_s, old))

    def send_tokens(r):
        for d in Y_ORDER:
            remote(zs.at[r, y_peer(d)], zr.at[r, yi], 0, y_sem.at[r], y_id(y_peer(d)))

    embed(0)
    wide_copy.wait()
    pl.semaphore_wait(barrier, len(Y_ORDER) + len(Z_ORDER) + len(X_ORDER))

    def to_modes(r):
        pltpu.make_async_copy(zr.at[r, 0 : NY - 1], zr.at[r, 0 : NY - 1], y_sem.at[r]).wait()
        z = zr[r].reshape(NY * PAD, CH).astype(F32)
        n = (z * gain_ref[:, channels] + shift_ref[:, channels]).astype(BF)
        s = (dot(wide[0], n) + dot(wide[1], n)).reshape(NZ * NX, 2 * MODES, CH)
        s = jnp.concatenate([s[:, :, 0:128], s[:, :, 128:256]], axis=1).astype(BF)
        s = s.reshape(NZ, NX, 16, 128)
        for x in range(NX):
            sb[x, r] = s[:, x]

    def some_rows(groups, g):
        return pl.ds(groups[g][0], groups[g][1] - groups[g][0])

    def send_modes(g):
        rows = some_rows(OUT_GROUPS, g)
        for d in Z_ORDER:
            remote(sb.at[:, rows, z_peer(d)], zr1.at[:, rows, zi], 1, z1_sem.at[g], z_id(z_peer(d)))
        pltpu.make_async_copy(sb.at[:, rows, zi], zr1.at[:, rows, zi], z1_sem.at[g]).start()

    def pass_on(g):
        rows = some_rows(OUT_GROUPS, g)
        pltpu.make_async_copy(zr1.at[:, rows], zr1.at[:, rows], z1_sem.at[g]).wait()
        for d in X_ORDER:
            remote(zr1.at[x_peer(d), rows], xr1.at[xi, rows], 2, x1_sem.at[g], x_id(x_peer(d)))
        pltpu.make_async_copy(zr1.at[xi, rows], xr1.at[xi, rows], x1_sem.at[g]).start()

    def mix(s):
        rows = pl.ds(s * RS, RS)
        for g, (low, _) in enumerate(OUT_GROUPS):
            if low // RS == s:
                some = some_rows(OUT_GROUPS, g)
                pltpu.make_async_copy(xr1.at[:, some], xr1.at[:, some], x1_sem.at[g]).wait()
        n = RS * NZ * 16
        for x in range(NX):
            rel[x * n : (x + 1) * n, :] = xr1[x, rows].astype(F32).reshape(n, 128)
        outs = []
        for k in range(2):
            cols = []
            for m in range(MODES):
                both = [rel[pl.ds(k * 8 + m * 2 + i, H, stride=16), :].astype(BF) for i in range(2)]
                cols.append(jnp.concatenate(both, axis=0))
            data = jnp.concatenate(cols, axis=1)
            g = dot(wide[2], data) + dot(wide[3], data)
            v = jnp.concatenate(
                [
                    jnp.concatenate([g[0:128, m * 128 : (m + 1) * 128], g[128:256, m * 128 : (m + 1) * 128]], axis=1)
                    for m in range(MODES)
                ],
                axis=0,
            )
            for first, (wh, wl, b_ref) in enumerate(((w1h, w1l, b1_ref), (w2h, w2l, b2_ref))):
                vh, vl = halves(v)
                bias = jnp.concatenate([b_ref[0, k : k + 1], b_ref[1, k : k + 1]], axis=1)
                v = dot(vh, wh[k]) + dot(vl, wh[k]) + dot(vh, wl[k]) + bias
                if first == 0:
                    v = jnp.maximum(v, 0.0)
            v = v - jnp.clip(v, -SHRINK, SHRINK)
            f = lax.broadcasted_iota(jnp.int32, (128, 1), 0)
            f = jnp.where(f < KEEP_LAT, f, 2 * KEEP_LAT - f)
            keep_lat = f < latc[k]
            cols = []
            for m in range(MODES):
                part = v[m * 128 : (m + 1) * 128]
                keep = jnp.logical_and(keep_lat, space * MODES + m < lonc[k])
                part = jnp.where(keep, part, 0.0)
                cols.append(jnp.concatenate([part[:, 0:128], part[:, 128:256]], axis=0))
            oh = jnp.concatenate(cols, axis=1).astype(BF)
            outs.append(dot(tall[0], oh) + dot(tall[1], oh))
        for k in range(2):
            for m in range(MODES):
                for i in range(2):
                    rel[pl.ds(k * 8 + m * 2 + i, H, stride=16), :] = outs[k][
                        i * H : (i + 1) * H, m * 128 : (m + 1) * 128
                    ]
        for x in range(NX):
            xs2[x, rows] = rel[x * n : (x + 1) * n, :].reshape(RS, NZ, 16, 128).astype(BF)
        for j, (low, _) in enumerate(BACK_GROUPS):
            if low // RS == s:
                some = some_rows(BACK_GROUPS, j)
                for d in X_ORDER:
                    remote(xs2.at[x_peer(d), some], xr2.at[xi, some], 3, x2_sem.at[j], x_id(x_peer(d)))
                pltpu.make_async_copy(xs2.at[xi, some], xr2.at[xi, some], x2_sem.at[j]).start()

    def send_back(j):
        some = some_rows(BACK_GROUPS, j)
        pltpu.make_async_copy(xr2.at[:, some], xr2.at[:, some], x2_sem.at[j]).wait()
        for d in Z_ORDER:
            remote(xr2.at[:, some, z_peer(d)], fr.at[:, some, zi], 4, z2_sem.at[j], z_id(z_peer(d)))
        pltpu.make_async_copy(xr2.at[:, some, zi], fr.at[:, some, zi], z2_sem.at[j]).start()

    def out_copy(r):
        return pltpu.make_async_copy(ob.at[r], out_hbm.at[r], out_sem)

    def to_tokens(r):
        a = fr[:, r].astype(F32).reshape(NX * NZ, 16, 128)
        a = jnp.concatenate([a[:, 0:8], a[:, 8:16]], axis=2).reshape(2 * KEEP_LON, CH).astype(BF)
        filtered = dot(tall[2], a) + dot(tall[3], a)
        for q in range(NY):
            stat = st[q]
            std = jnp.sum(jnp.where(lane == 2 * r, stat, 0.0), axis=1, keepdims=True)
            mean = jnp.sum(jnp.where(lane == 2 * r + 1, stat, 0.0), axis=1, keepdims=True)
            mixed = filtered[q * PAD : (q + 1) * PAD] + (zr[r, q].astype(F32) * std + mean)
            flat[q * COLS : (q + 1) * COLS, :] = mixed[0:COLS]
        ob[r] = flat[...].astype(BF)
        out_copy(r).start()

    @pl.loop(0, ROWS + LAG)
    def _(i):
        @pl.when(i < ROWS)
        def _():
            send_tokens(i)

        @pl.when(i < RS - 1)
        def _():
            embed(i + 1)

        @pl.when(i == RS)
        def _():
            w1_copy.wait()
            w2_copy.wait()
            for k in range(2):
                w1h[k], w1l[k] = halves(complex_weight(w1_ref, k))
                w2h[k], w2l[k] = halves(complex_weight(w2_ref, k))

        @pl.when(i == ROWS - 1)
        def _():
            for d in Y_ORDER:
                remote(st.at[yi], st.at[yi], 5, st_sem, y_id(y_peer(d)))

        @pl.when(i >= LAG)
        def _():
            to_modes(i - LAG)

        for g, (_, high) in enumerate(OUT_GROUPS):
            pl.when(i == LAG + high - 1)(functools.partial(send_modes, g))
            if high + FWD <= ROWS:
                pl.when(i == LAG + high - 1 + FWD)(functools.partial(pass_on, g))

    tall_copy.wait()
    mix(0)
    pass_on(5)
    send_back(0)
    send_back(1)
    pass_on(6)
    send_back(2)
    pass_on(7)
    mix(1)
    send_back(3)
    pltpu.make_async_copy(st.at[0 : NY - 1], st.at[0 : NY - 1], st_sem).wait()

    @pl.loop(0, ROWS)
    def _(r):
        for j, (low, _) in enumerate(BACK_GROUPS):

            @pl.when(r == low)
            def _(j=j):
                some = some_rows(BACK_GROUPS, j)
                pltpu.make_async_copy(fr.at[:, some], fr.at[:, some], z2_sem.at[j]).wait()

        to_tokens(r)
        for j in range(4, len(BACK_GROUPS)):
            pl.when(r == j - 4)(functools.partial(send_back, j))

    for sends, ref in enumerate(
        (
            zs.at[:, 0 : NY - 1],
            sb.at[:, :, 0 : NZ - 1],
            zr1.at[0 : NX - 1],
            xs2.at[0 : NX - 1],
            xr2.at[:, :, 0 : NZ - 1],
            st.at[0 : NY - 1],
        )
    ):
        pltpu.make_async_copy(ref, ref, send_sem.at[sends]).wait()
    pltpu.make_async_copy(ob, out_hbm, out_sem).wait()


def copy_rows(src, dst, held, in_sem, out_sem):
    pieces = [pl.ds(i * COPY, COPY) for i in range(ROWS // COPY)]
    for i, rows in enumerate(pieces):
        pltpu.make_async_copy(src.at[rows], held.at[rows], in_sem.at[i]).start()
    for i, rows in enumerate(pieces):
        pltpu.make_async_copy(src.at[rows], held.at[rows], in_sem.at[i]).wait()
        pltpu.make_async_copy(held.at[rows], dst.at[rows], out_sem.at[i]).start()
    for i, rows in enumerate(pieces):
        pltpu.make_async_copy(held.at[rows], dst.at[rows], out_sem.at[i]).wait()


def solution(mesh):
    wide, tall = phase_tables()

    def local(
        patches, embed_weight, embed_bias, norm_gain, norm_bias, w_one, b_one, w_two, b_two, lat_cut, lon_cut
    ):
        anywhere = pl.BlockSpec(memory_space=pltpu.HBM)
        vmem = pl.BlockSpec(memory_space=pltpu.VMEM)
        smem = pl.BlockSpec(memory_space=pltpu.SMEM)
        back = (NX, ROWS, NZ, 16, 128)
        out = pl.pallas_call(
            kernel,
            out_shape=jax.ShapeDtypeStruct((ROWS, W, CH), BF),
            in_specs=[anywhere, anywhere, vmem, vmem, vmem, anywhere, vmem, anywhere, vmem, smem, smem, anywhere, anywhere],
            out_specs=pl.BlockSpec(memory_space=pl.ANY),
            scratch_shapes=[
                pltpu.VMEM((RS, PARTS, COLS, SAMPLES, LANES), BF),
                pltpu.VMEM((2 * COLS, PATCH), BF),
                pltpu.VMEM((D // LANES + 1, 2 * COLS, LANES), F32),
                pltpu.VMEM((PATCH, D), BF),
                pltpu.VMEM((2, 2, 128, 128), F32),
                pltpu.VMEM((2, 2, 128, 128), F32),
                pltpu.VMEM((4, 256, 384), BF),
                pltpu.VMEM((4, 384, 256), BF),
                pltpu.VMEM((ROWS, NY, PAD, CH), BF),
                pltpu.VMEM((ROWS, NY, PAD, CH), BF),
                pltpu.VMEM((NY, PAD, 128), F32),
                pltpu.VMEM(back, BF),
                pltpu.VMEM(back, BF),
                pltpu.VMEM(back, BF),
                pltpu.VMEM((H * 16, 128), F32),
                pltpu.VMEM(back, BF),
                pltpu.VMEM(back, BF),
                pltpu.VMEM(back, BF),
                pltpu.VMEM((ROWS, W, CH), BF),
                pltpu.VMEM((W, CH), F32),
            ]
            + [pltpu.VMEM((2, 256, 256), BF)] * 4
            + [
                pltpu.SemaphoreType.DMA((RS,)),
                pltpu.SemaphoreType.DMA,
                pltpu.SemaphoreType.DMA((4,)),
                pltpu.SemaphoreType.DMA((6,)),
                pltpu.SemaphoreType.DMA((ROWS,)),
                pltpu.SemaphoreType.DMA,
                pltpu.SemaphoreType.DMA((len(OUT_GROUPS),)),
                pltpu.SemaphoreType.DMA((len(OUT_GROUPS),)),
                pltpu.SemaphoreType.DMA((len(BACK_GROUPS),)),
                pltpu.SemaphoreType.DMA((len(BACK_GROUPS),)),
                pltpu.SemaphoreType.DMA,
            ],
            compiler_params=pltpu.CompilerParams(
                collective_id=0, has_side_effects=True, vmem_limit_bytes=54 * 1024 * 1024
            ),
            name="afno",
        )(
            patches.reshape(SAMPLES, RS, COLS, PARTS, LANES).transpose(1, 2, 3, 0, 4),
            embed_weight,
            embed_bias.reshape(1, D),
            norm_gain.reshape(1, D),
            norm_bias.reshape(1, D),
            w_one,
            b_one,
            w_two,
            b_two,
            lat_cut,
            lon_cut,
            jnp.asarray(wide),
            jnp.asarray(tall),
        )
        out = pl.pallas_call(
            copy_rows,
            out_shape=jax.ShapeDtypeStruct((ROWS, W, CH), BF),
            in_specs=[anywhere],
            out_specs=pl.BlockSpec(memory_space=pl.ANY),
            scratch_shapes=[
                pltpu.VMEM((ROWS, W, CH), BF),
                pltpu.SemaphoreType.DMA((ROWS,)),
                pltpu.SemaphoreType.DMA((ROWS,)),
            ],
            name="copy_rows",
        )(out)
        return out.reshape(SAMPLES, RS, W, CH)

    in_specs = (
        P("dp", "space", "feat", None),
        P(),
        P(),
        P(),
        P(),
        P(None, "feat", None, None),
        P(None, "feat", None),
        P(None, "feat", None, None),
        P(None, "feat", None),
        P("feat"),
        P("feat"),
    )
    return jax.shard_map(
        local, mesh=mesh, in_specs=in_specs, out_specs=P("dp", "space", None, "feat"), check_vma=False
    )
```
